768 devices in a mesh: blk: 24 (over x, z_hi, core), sub: 32 (over z_lo, y).
Axes of the slice: x: 4, y: 8, z: 12 (z_hi: 3, z_lo: 4; z = z_hi * 4 + z_lo), core: 2. Of those that a mesh axis runs over, the one named last changes fastest.
Arguments:
- images: bfloat16 [196608, 1152], P(('blk', 'sub')), may hold values from -280 to 280
- texts: bfloat16 [196608, 1152], P(('blk', 'sub')), may hold values from -280 to 280
- log_temp: float32 [1], replicated, may hold values from 1.4 to 2.5
- bias: float32 [1], replicated, may hold values from -4 to -1
Outputs:
- loss: float32 [1], replicated
- image_grad: bfloat16 [196608, 1152], P(('blk', 'sub'))
- text_grad: bfloat16 [196608, 1152], P(('blk', 'sub'))
- temp_grad: float32 [1], replicated
- bias_grad: float32 [1], replicated
The draws below stay inside these ranges and needn't reach their ends.
All inputs are finite; a program needn't handle non-finite values.
Results may differ from the reference program's by a relative error of at most 0.0034.
Values may be sent and summed in bfloat16 or wider, within the bound.
No kernel may reach another device: no remote copies, remote signals or barrier semaphores. Data moves between devices by JAX's collectives and lax.ppermute only.
A program may use at most 32 MiB of HBM per device.

```python
import jax
import jax.numpy as jnp
from jax import lax

D = 1152
TOK_DEV = 256
GROUPS = 4
TOKENS = 196608


def shared_parts(key):
    common = jnp.clip(jax.random.normal(jax.random.fold_in(key, 101), (D,), jnp.float32), -4.0, 4.0)
    shared = jnp.clip(jax.random.normal(jax.random.fold_in(key, 102), (TOKENS, D), jnp.float32), -4.0, 4.0)
    block_level = jax.random.uniform(jax.random.fold_in(key, 103), (TOKENS // TOK_DEV,), jnp.float32, 0.0, 1.0)
    row_block = jnp.arange(TOKENS, dtype=jnp.int32) // TOK_DEV
    position = block_level[row_block]
    return (common, shared, position)


def build_rows(base_key, own_key, own, slope, top):
    common, shared, position = shared_parts(base_key)
    level = slope * position
    scale = jnp.exp(jax.random.uniform(jax.random.fold_in(own_key, 7), (TOKENS, 1), jnp.float32, 0.0, jnp.log(top)))
    return scale * (level[:, None] * common[None, :] + shared + 0.7 * own)


def draw_images(key, part):
    own_key = jax.random.fold_in(key, 1)
    own = jnp.clip(jax.random.normal(own_key, (TOKENS, D), jnp.float32), -4.0, 4.0)
    values = build_rows(key, own_key, own, 2.5, 10.0)
    return values.astype(jnp.bfloat16)


def draw_texts(key, part):
    own_key = jax.random.fold_in(key, 2)
    own = jnp.clip(jax.random.normal(own_key, (TOKENS, D), jnp.float32), -4.0, 4.0)
    values = build_rows(key, own_key, own, 2.5, 10.0)
    return values.astype(jnp.bfloat16)


def setup_inputs(seed: int = 0) -> dict:
    keys = jax.random.split(jax.random.key(seed), 5)
    images = draw_images(jax.random.fold_in(keys[4], 71), 0)
    texts = draw_texts(jax.random.fold_in(keys[4], 71), 0)
    log_temp = jnp.clip(jax.random.uniform(keys[2], (1,), jnp.float32, 1.4, 2.5), 1.4, 2.5)
    bias = jnp.clip(jax.random.uniform(keys[3], (1,), jnp.float32, -4.0, -1.0), -4.0, -1.0)
    return dict(images=images, texts=texts, log_temp=log_temp, bias=bias)


def unit_rows(values):
    wide = values.astype(jnp.float32)
    norm = jnp.sqrt(lax.optimization_barrier(jnp.sum(wide * wide, axis=1, keepdims=True)) + 1e-06)
    return (wide / norm, norm)

def score_group(img_b, block, temp, shift_b, first):
    cos = lax.dot_general(img_b, block, (((1,), (1,)), ((), ())), preferred_element_type=jnp.float32)
    logit = temp * cos + shift_b
    rows = img_b.shape[0]
    if first:
        sign = jnp.where(jnp.eye(rows, dtype=bool), jnp.float32(1.0), jnp.float32(-1.0))
    else:
        sign = jnp.full((rows, rows), -1.0, jnp.float32)
    loss = -jnp.sum(jax.nn.log_sigmoid(sign * logit))
    grad = -sign * jax.nn.sigmoid(-sign * logit)
    dtemp = temp * jnp.sum(grad * cos)
    dbias = jnp.sum(grad)
    grad_b = grad.astype(jnp.bfloat16)
    dimg = temp * jnp.dot(grad_b, block, preferred_element_type=jnp.float32)
    dtxt = temp * lax.dot_general(grad_b, img_b, (((0,), (0,)), ((), ())), preferred_element_type=jnp.float32)
    return (dimg, dtxt, loss, dtemp, dbias)

def reference(images, texts, log_temp, bias):
    blocks = TOKENS // TOK_DEV
    img_unit, img_norm = unit_rows(images)
    txt_unit, txt_norm = unit_rows(texts)
    img_b = img_unit.astype(jnp.bfloat16)
    txt_b = txt_unit.astype(jnp.bfloat16)
    temp = jnp.exp(log_temp[0])
    shift_b = bias[0]

    def step(accum, index):
        start = (index * TOK_DEV).astype(jnp.int32)
        own_b = lax.dynamic_slice_in_dim(img_b, start, TOK_DEV, 0)
        own_unit = lax.dynamic_slice_in_dim(img_unit, start, TOK_DEV, 0)
        own_norm = lax.dynamic_slice_in_dim(img_norm, start, TOK_DEV, 0)
        img_dir = jnp.zeros((TOK_DEV, D), jnp.float32)
        loss = jnp.zeros((), jnp.float32)
        dtemp = jnp.zeros((), jnp.float32)
        dbias = jnp.zeros((), jnp.float32)
        for group in range(GROUPS):
            other = ((index - group + blocks) % blocks).astype(jnp.int32) * TOK_DEV
            block = lax.dynamic_slice_in_dim(txt_b, other, TOK_DEV, 0)
            dimg, dtxt, part, dt_part, db_part = score_group(own_b, block, temp, shift_b, group == 0)
            img_dir = img_dir + dimg
            loss = loss + part
            dtemp = dtemp + dt_part
            dbias = dbias + db_part
            current = lax.dynamic_slice_in_dim(accum, other, TOK_DEV, 0)
            accum = lax.dynamic_update_slice_in_dim(accum, current + dtxt, other, 0)
        along = lax.optimization_barrier(jnp.sum(own_unit * img_dir, axis=1, keepdims=True))
        grad_rows = ((img_dir - own_unit * along) / own_norm).astype(jnp.bfloat16)
        return (accum, (grad_rows, loss, dtemp, dbias))
    start_acc = jnp.zeros((TOKENS, D), jnp.float32)
    txt_dir, outputs = lax.scan(step, start_acc, jnp.arange(blocks, dtype=jnp.int32))
    grad_rows, losses, dtemps, dbiases = outputs
    image_grad = grad_rows.reshape(TOKENS, D)
    along = lax.optimization_barrier(jnp.sum(txt_unit * txt_dir, axis=1, keepdims=True))
    text_grad = ((txt_dir - txt_unit * along) / txt_norm).astype(jnp.bfloat16)
    loss = (jnp.sum(losses) / TOKENS).reshape(1)
    temp_grad = (jnp.sum(dtemps) / TOKENS).reshape(1)
    bias_grad = (jnp.sum(dbiases) / TOKENS).reshape(1)
    return (loss, image_grad, text_grad, temp_grad, bias_grad)
```

```python
import jax
import jax.numpy as jnp
from jax import lax
from jax.sharding import PartitionSpec as P

AXES = ("blk", "sub")


def from_behind(value, steps):
    count = lax.axis_size(AXES)
    pairs = [(source, (source + steps) % count) for source in range(count)]
    return lax.ppermute(value, AXES, pairs)


def unit_rows(values):
    wide = values.astype(jnp.float32)
    norm = jnp.sqrt(jnp.sum(wide * wide, axis=1, keepdims=True) + 1e-06)
    return (wide / norm, norm)


def unit_b(values):
    return unit_rows(values)[0].astype(jnp.bfloat16)


def scores(left, right, temp, shift_b, first):
    cos = lax.dot_general(
        left, right, (((1,), (1,)), ((), ())), preferred_element_type=jnp.float32
    )
    z = temp * cos + shift_b
    if first:
        eye = jnp.eye(left.shape[0], dtype=bool)
        z = jnp.where(eye, -z, z)
    e = jnp.exp(-jnp.abs(z))
    grad = jnp.where(z >= 0, 1.0, e) / (1.0 + e)
    if first:
        grad = jnp.where(eye, -grad, grad)
    loss = jnp.maximum(z, 0.0) + jnp.log1p(e)
    return cos, grad, loss


def fold(values):
    return jnp.sum(values, axis=0)


def tally(cos, grad, loss):
    return jnp.stack([fold(loss), fold(grad * cos), fold(grad)])


def pull(grad, other):
    return jnp.dot(grad.astype(jnp.bfloat16), other, preferred_element_type=jnp.float32)


def total_over(part, axis):
    count = lax.axis_size(axis)
    copies = jnp.broadcast_to(part[None], (count,) + part.shape)
    return jnp.sum(lax.all_to_all(copies, axis, 0, 0, tiled=True), axis=0)


def norm_back(unit, norm, direction):
    along = jnp.sum(unit * direction, axis=1, keepdims=True)
    return ((direction - unit * along) / norm).astype(jnp.bfloat16)


def per_device(images, texts, log_temp, bias):
    rows = images.shape[0]
    total = rows * lax.axis_size(AXES)
    t1 = from_behind(texts, 1)
    i1 = from_behind(images, -1)
    t2 = from_behind(t1, 1)
    i2 = from_behind(i1, -1)
    t3 = from_behind(t2, 1)
    i3 = from_behind(i2, -1)
    temp = jnp.exp(log_temp[0])
    shift_b = bias[0]
    img_unit, img_norm = unit_rows(images)
    txt_unit, txt_norm = unit_rows(texts)
    img_b = img_unit.astype(jnp.bfloat16)
    txt_b = txt_unit.astype(jnp.bfloat16)

    cos, grad, loss = scores(img_b, txt_b, temp, shift_b, True)
    sums = tally(cos, grad, loss)
    img_dir = pull(grad, txt_b)
    txt_dir = lax.dot_general(
        grad.astype(jnp.bfloat16), img_b, (((0,), (0,)), ((), ())),
        preferred_element_type=jnp.float32,
    )
    i1_b = None
    for text, image, step in ((t1, i1, 1), (t2, i2, 2), (t3, i3, 3)):
        text_b = unit_b(text)
        image_b = unit_b(image)
        cos, grad, loss = scores(img_b, text_b, temp, shift_b, False)
        if step < 3:
            sums = sums + tally(cos, grad, loss)
        if step == 1:
            i1_b = image_b
        if step == 2:
            sums = sums + tally(*scores(i1_b, text_b, temp, shift_b, False))
        img_dir = img_dir + pull(grad, text_b)
        cos, grad, loss = scores(txt_b, image_b, temp, shift_b, False)
        txt_dir = txt_dir + pull(grad, image_b)

    part = jnp.pad(sums[:, :128] + sums[:, 128:], ((0, 5), (0, 0)))
    part = total_over(total_over(part, "sub"), "blk")
    part = jnp.sum(part, axis=1)
    image_grad = norm_back(img_unit, img_norm, temp * img_dir)
    text_grad = norm_back(txt_unit, txt_norm, temp * txt_dir)
    loss_out = (part[0] / total).reshape(1)
    temp_grad = (temp * part[1] / total).reshape(1)
    bias_grad = (part[2] / total).reshape(1)
    return (loss_out, image_grad, text_grad, temp_grad, bias_grad)


def solution(mesh):
    in_specs = (P(AXES, None), P(AXES, None), P(), P())
    out_specs = (P(), P(AXES, None), P(AXES, None), P(), P())
    return jax.shard_map(
        per_device, mesh=mesh, in_specs=in_specs, out_specs=out_specs, check_vma=False
    )
```

```python
import functools

import jax
import jax.numpy as jnp
from jax import lax
from jax.experimental import pallas as pl
from jax.experimental.pallas import tpu as pltpu
from jax.sharding import PartitionSpec as P

AXES = ("blk", "sub")
ROWS = 64
VMEM = pl.BlockSpec(memory_space=pltpu.VMEM)
ANY = pl.BlockSpec(memory_space=pl.ANY)
SMEM = pl.BlockSpec(memory_space=pltpu.SMEM)
F32 = jnp.float32
BF16 = jnp.bfloat16


def swap_ahead(value):
    count = lax.axis_size(AXES)
    return lax.ppermute(value, AXES, [(at, at ^ 1) for at in range(count)])


def swap_across(value):
    count = lax.axis_size(AXES)
    pairs = [(at, (at - 1 if at % 2 == 0 else at + 1) % count) for at in range(count)]
    return lax.ppermute(value, AXES, pairs)


def is_even():
    return lax.axis_index("sub") % 2 == 0


def chunks(ref, size=ROWS):
    return [pl.ds(start, size) for start in range(0, ref.shape[0], size)]


def inverse_norm(wide):
    return 1.0 / jnp.sqrt(jnp.sum(wide * wide, axis=1, keepdims=True) + 1e-06)


def unit_into(out_ref, in_ref):
    for rows in chunks(in_ref, 32):
        wide = in_ref[rows, :].astype(F32)
        out_ref[rows, :] = (wide * inverse_norm(wide)).astype(BF16)


def cosines(left, right):
    return lax.dot_general(left, right, (((1,), (1,)), ((), ())), preferred_element_type=F32)


def score(cos, temp, shift_b, diagonal=None):
    z = temp * cos + shift_b
    if diagonal is not None:
        row = lax.broadcasted_iota(jnp.int32, z.shape, 0) + diagonal
        eye = row == lax.broadcasted_iota(jnp.int32, z.shape, 1)
        z = jnp.where(eye, -z, z)
    e = jnp.exp(-jnp.abs(z))
    r = 1.0 / (1.0 + e)
    grad = jnp.where(z >= 0, r, e * r)
    if diagonal is not None:
        grad = jnp.where(eye, -grad, grad)
    return cos, z, e, grad


def fold(values):
    rows = values.shape[0]
    part = jnp.sum(values.reshape(rows // 8, 8, values.shape[1]), axis=0)
    return sum(part[:, at : at + 128] for at in range(0, values.shape[1], 128))


def tally(cos, z, e, grad):
    rows, columns = e.shape
    factors = (1.0 + e).reshape(rows // 8, 8, columns)
    product = factors[0]
    for at in range(1, rows // 8):
        product = product * factors[at]
    return (
        fold(jnp.maximum(z, 0.0)) + fold(jnp.log(product)),
        fold(grad * cos),
        fold(grad),
    )


def add3(left, right):
    return tuple(a + b for a, b in zip(left, right))


def pack(sums):
    row = lax.broadcasted_iota(jnp.int32, (8, 128), 0)
    loss, dtemp, dbias = (jnp.sum(part, axis=0, keepdims=True) for part in sums)
    rest = jnp.where(row == 2, dbias, 0.0)
    return jnp.where(row == 0, loss, jnp.where(row == 1, dtemp, rest))


def zero3():
    return (jnp.zeros((8, 128), F32),) * 3


def score_all(cos_ref, g_ref, temp, shift_b, own=False, sums=None):
    for rows in chunks(cos_ref, ROWS):
        terms = score(cos_ref[rows, :], temp, shift_b, rows.start if own else None)
        if sums is not None:
            sums = add3(sums, tally(*terms))
        if g_ref is not None:
            g_ref[rows, :] = terms[3].astype(BF16)
    return sums


def pull(g_ref, other_ref):
    return jnp.dot(g_ref[...], other_ref[...], preferred_element_type=F32)


def order_kernel(images, texts, a, b, sem):
    def move(first, second):
        copies = [
            pltpu.make_async_copy(first, a, sem.at[0]),
            pltpu.make_async_copy(second, b, sem.at[1]),
        ]
        for copy in copies:
            copy.start()
        for copy in copies:
            copy.wait()

    even = is_even()
    pl.when(even)(lambda: move(texts, images))
    pl.when(jnp.logical_not(even))(lambda: move(images, texts))


def own_kernel(a, b, temp_ref, bias_ref, a_b, b_b, dir_a, dir_b, sums_ref, cos_ref, g_ref):
    temp, shift_b = temp_ref[0], bias_ref[0]
    unit_into(a_b, a)
    unit_into(b_b, b)
    cos_ref[...] = cosines(a_b[...], b_b[...])
    sums_ref[...] = pack(score_all(cos_ref, g_ref, temp, shift_b, True, zero3()))
    dir_a[...] = pull(g_ref, b_b)
    cos_ref[...] = cosines(b_b[...], a_b[...])
    score_all(cos_ref, g_ref, temp, shift_b, True)
    dir_b[...] = pull(g_ref, a_b)


def next_kernel(
    ra, rb, a_b, b_b, dir_a_in, dir_b_in, sums_in, temp_ref, bias_ref,
    dir_a, dir_b, ra_b, rb_b, sums_ref, cos_ref, g_ref,
):
    temp, shift_b = temp_ref[0], bias_ref[0]
    sums = zero3()
    for raw, raw_b, own_b, start, out in (
        (ra, ra_b, a_b, dir_a_in, dir_a),
        (rb, rb_b, b_b, dir_b_in, dir_b),
    ):
        unit_into(raw_b, raw)
        cos_ref[...] = cosines(own_b[...], raw_b[...])
        sums = score_all(cos_ref, g_ref, temp, shift_b, False, sums)
        out[...] = start[...] + pull(g_ref, raw_b)
    sums_ref[...] = sums_in[...] + 0.5 * pack(sums)


def sums_kernel(
    ra2, rb2, a_b, b_b, ra_b, rb_b, sums_in, temp_ref, bias_ref, copies, far_b, cos_ref
):
    temp, shift_b = temp_ref[0], bias_ref[0]

    def run(far, own_b, near_b):
        unit_into(far_b, far)
        sums = zero3()
        for ref in (own_b, near_b):
            cos_ref[...] = cosines(ref[...], far_b[...])
            sums = score_all(cos_ref, None, temp, shift_b, False, sums)
        packed = sums_in[...] + pack(sums)
        for at in range(copies.shape[0]):
            copies[at] = packed

    even = is_even()
    pl.when(even)(lambda: run(rb2, b_b, ra_b))
    pl.when(jnp.logical_not(even))(lambda: run(ra2, a_b, rb_b))


def far_direction(dir_ref, start, own_b, raws, units, grads, cos_ref, temp, shift_b):
    for raw, unit_b, g_ref in zip(raws, units, grads):
        unit_into(unit_b, raw)
        cos_ref[...] = cosines(own_b[...], unit_b[...])
        score_all(cos_ref, g_ref, temp, shift_b)
    dir_ref[...] = start[...] + pull(grads[0], units[0]) + pull(grads[1], units[1])


def back_into(out_ref, own_ref, dir_ref, temp):
    for rows in chunks(out_ref, 32):
        wide = own_ref[rows, :].astype(F32)
        direction = dir_ref[rows, :]
        inverse = inverse_norm(wide)
        unit = wide * inverse
        along = jnp.sum(unit * direction, axis=1, keepdims=True)
        out_ref[rows, :] = ((direction - unit * along) * (temp * inverse)).astype(BF16)


def first_kernel(
    ra2, ra3, a, a_b, dir_a, temp_ref, bias_ref, grad_a,
    u2, u3, cos_ref, g2, g3, dir_ref,
):
    temp, shift_b = temp_ref[0], bias_ref[0]
    far_direction(dir_ref, dir_a, a_b, (ra2, ra3), (u2, u3), (g2, g3), cos_ref, temp, shift_b)
    back_into(grad_a, a, dir_ref, temp)


def second_kernel(
    rb2, rb3, b, b_b, dir_b, grad_a, temp_ref, bias_ref, image_grad, text_grad,
    u2, u3, cos_ref, g2, g3, dir_ref, grad_b, sem,
):
    temp, shift_b = temp_ref[0], bias_ref[0]
    far_direction(dir_ref, dir_b, b_b, (rb2, rb3), (u2, u3), (g2, g3), cos_ref, temp, shift_b)
    back_into(grad_b, b, dir_ref, temp)

    def move(first, second):
        copies = [
            pltpu.make_async_copy(grad_a, first, sem.at[0]),
            pltpu.make_async_copy(grad_b, second, sem.at[1]),
        ]
        for copy in copies:
            copy.start()
        for copy in copies:
            copy.wait()

    even = is_even()
    pl.when(even)(lambda: move(text_grad, image_grad))
    pl.when(jnp.logical_not(even))(lambda: move(image_grad, text_grad))


def add_parts(parts):
    packed = parts[0]
    for at in range(1, parts.shape[0]):
        packed = packed + parts[at]
    return packed


def relay_kernel(parts, copies):
    packed = add_parts(parts)
    for at in range(copies.shape[0]):
        copies[at] = packed


def finish_kernel(total, parts, temp_ref, loss, dtemp, dbias):
    packed = add_parts(parts)
    loss[0] = jnp.sum(packed[0:1, :]) / total
    dtemp[0] = temp_ref[0] * jnp.sum(packed[1:2, :]) / total
    dbias[0] = jnp.sum(packed[2:3, :]) / total


def call(kernel, ins, outs, out_specs, scratch=(), matmuls=0, spec=VMEM):
    specs = [SMEM if value.shape == (1,) else spec for value in ins]
    return pl.pallas_call(
        kernel,
        out_shape=outs,
        in_specs=specs,
        out_specs=out_specs,
        scratch_shapes=list(scratch),
        compiler_params=pltpu.CompilerParams(vmem_limit_bytes=12 * 2**20),
        cost_estimate=pl.CostEstimate(
            flops=matmuls * 2 * 256 * 256 * 1152, bytes_accessed=2**20, transcendentals=0
        ),
    )(*ins)


def per_device(images, texts, log_temp, bias):
    shape = images.shape
    rows = shape[0]
    total = rows * lax.axis_size(AXES)
    wide = jax.ShapeDtypeStruct(shape, F32)
    half = jax.ShapeDtypeStruct(shape, BF16)
    tile = jax.ShapeDtypeStruct((8, 128), F32)
    one = jax.ShapeDtypeStruct((1,), F32)
    unit, direction = pltpu.VMEM(shape, BF16), pltpu.VMEM(shape, F32)
    cos, grad = pltpu.VMEM((rows, rows), F32), pltpu.VMEM((rows, rows), BF16)
    pair_sem = pltpu.SemaphoreType.DMA((2,))
    temp = jnp.exp(log_temp)

    a, b = call(order_kernel, (images, texts), (half, half), (VMEM, VMEM), (pair_sem,), 0, ANY)
    ra, rb = swap_ahead(a), swap_across(b)
    own = call(
        own_kernel, (a, b, temp, bias), (half, half, wide, wide, tile), (VMEM,) * 5,
        (cos, grad), 8,
    )
    ra, rb, (a_b, b_b, dir_a, dir_b, sums) = lax.optimization_barrier((ra, rb, own))
    ra2, rb2 = swap_ahead(rb), swap_across(ra)
    near = call(
        next_kernel, (ra, rb, a_b, b_b, dir_a, dir_b, sums, temp, bias),
        (wide, wide, half, half, tile), (VMEM,) * 5, (cos, grad), 8,
    )
    ra2, rb2, (dir_a, dir_b, ra_b, rb_b, sums) = lax.optimization_barrier((ra2, rb2, near))
    ra3, rb3 = swap_ahead(rb2), swap_across(ra2)
    copies = call(
        sums_kernel, (ra2, rb2, a_b, b_b, ra_b, rb_b, sums, temp, bias),
        jax.ShapeDtypeStruct((lax.axis_size("blk"), 8, 128), F32), VMEM, (unit, cos), 4,
    )
    parts = lax.all_to_all(copies, "blk", 0, 0, tiled=True)
    scratch = (unit, unit, cos, grad, grad, direction)
    grad_a = call(first_kernel, (ra2, ra3, a, a_b, dir_a, temp, bias), half, VMEM, scratch, 8)
    parts, grad_a = lax.optimization_barrier((parts, grad_a))
    copies = call(
        relay_kernel, (parts,), jax.ShapeDtypeStruct((lax.axis_size("sub"), 8, 128), F32), VMEM
    )
    dir_b, _ = lax.optimization_barrier((dir_b, copies))
    parts = lax.all_to_all(copies, "sub", 0, 0, tiled=True)
    image_grad, text_grad = call(
        second_kernel, (rb2, rb3, b, b_b, dir_b, grad_a, temp, bias), (half, half), (ANY, ANY),
        scratch + (unit, pair_sem), 8,
    )
    loss, dtemp, dbias = call(
        functools.partial(finish_kernel, total), (parts, temp), (one,) * 3, (SMEM,) * 3
    )
    return (loss, image_grad, text_grad, dtemp, dbias)


def solution(mesh):
    in_specs = (P(AXES, None), P(AXES, None), P(), P())
    out_specs = (P(), P(AXES, None), P(AXES, None), P(), P())
    return jax.shard_map(
        per_device, mesh=mesh, in_specs=in_specs, out_specs=out_specs, check_vma=False
    )
```

```python
import functools

import jax
import jax.numpy as jnp
from jax import lax
from jax.experimental import pallas as pl
from jax.experimental.pallas import tpu as pltpu
from jax.sharding import PartitionSpec as P

AXES = ("blk", "sub")
ROWS = 64
VMEM = pl.BlockSpec(memory_space=pltpu.VMEM)
ANY = pl.BlockSpec(memory_space=pl.ANY)
SMEM = pl.BlockSpec(memory_space=pltpu.SMEM)
F32 = jnp.float32
BF16 = jnp.bfloat16


def swap_ahead(value):
    count = lax.axis_size(AXES)
    return lax.ppermute(value, AXES, [(at, at ^ 1) for at in range(count)])


def swap_across(value):
    count = lax.axis_size(AXES)
    pairs = [(at, (at - 1 if at % 2 == 0 else at + 1) % count) for at in range(count)]
    return lax.ppermute(value, AXES, pairs)


def is_even():
    return lax.axis_index("sub") % 2 == 0


def chunks(ref, size=ROWS):
    return [pl.ds(start, size) for start in range(0, ref.shape[0], size)]


def inverse_norm(wide):
    return 1.0 / jnp.sqrt(jnp.sum(wide * wide, axis=1, keepdims=True) + 1e-06)


def unit_into(out_ref, in_ref):
    for rows in chunks(in_ref, 32):
        wide = in_ref[rows, :].astype(F32)
        out_ref[rows, :] = (wide * inverse_norm(wide)).astype(BF16)


def cosines(left, right):
    return lax.dot_general(left, right, (((1,), (1,)), ((), ())), preferred_element_type=F32)


def score(cos, temp, shift_b, diagonal=None):
    z = temp * cos + shift_b
    if diagonal is not None:
        row = lax.broadcasted_iota(jnp.int32, z.shape, 0) + diagonal
        eye = row == lax.broadcasted_iota(jnp.int32, z.shape, 1)
        z = jnp.where(eye, -z, z)
    e = jnp.exp(-jnp.abs(z))
    r = 1.0 / (1.0 + e)
    grad = jnp.where(z >= 0, r, e * r)
    if diagonal is not None:
        grad = jnp.where(eye, -grad, grad)
    return cos, z, e, grad


def fold(values):
    rows = values.shape[0]
    part = jnp.sum(values.reshape(rows // 8, 8, values.shape[1]), axis=0)
    return sum(part[:, at : at + 128] for at in range(0, values.shape[1], 128))


def tally(cos, z, e, grad):
    rows, columns = e.shape
    factors = (1.0 + e).reshape(rows // 8, 8, columns)
    product = factors[0]
    for at in range(1, rows // 8):
        product = product * factors[at]
    return (
        fold(jnp.maximum(z, 0.0)) + fold(jnp.log(product)),
        fold(grad * cos),
        fold(grad),
    )


def add3(left, right):
    return tuple(a + b for a, b in zip(left, right))


def pack(sums):
    row = lax.broadcasted_iota(jnp.int32, (8, 128), 0)
    loss, dtemp, dbias = (jnp.sum(part, axis=0, keepdims=True) for part in sums)
    rest = jnp.where(row == 2, dbias, 0.0)
    return jnp.where(row == 0, loss, jnp.where(row == 1, dtemp, rest))


def zero3():
    return (jnp.zeros((8, 128), F32),) * 3


def score_all(cos_ref, g_ref, temp, shift_b, own=False, sums=None):
    for rows in chunks(cos_ref, ROWS):
        terms = score(cos_ref[rows, :], temp, shift_b, rows.start if own else None)
        if sums is not None:
            sums = add3(sums, tally(*terms))
        if g_ref is not None:
            g_ref[rows, :] = terms[3].astype(BF16)
    return sums


def pull(g_ref, other_ref):
    return jnp.dot(g_ref[...], other_ref[...], preferred_element_type=F32)


def order_kernel(images, texts, a, b, sem):
    def move(first, second):
        copies = [
            pltpu.make_async_copy(first, a, sem.at[0]),
            pltpu.make_async_copy(second, b, sem.at[1]),
        ]
        for copy in copies:
            copy.start()
        for copy in copies:
            copy.wait()

    even = is_even()
    pl.when(even)(lambda: move(texts, images))
    pl.when(jnp.logical_not(even))(lambda: move(images, texts))


def own_kernel(a, b, temp_ref, bias_ref, a_b, b_b, dir_a, dir_b, sums_ref, cos_ref, g_ref):
    temp, shift_b = temp_ref[0], bias_ref[0]
    unit_into(a_b, a)
    unit_into(b_b, b)
    cos_ref[...] = cosines(a_b[...], b_b[...])
    sums_ref[...] = pack(score_all(cos_ref, g_ref, temp, shift_b, True, zero3()))
    dir_a[...] = pull(g_ref, b_b)
    cos_ref[...] = cosines(b_b[...], a_b[...])
    score_all(cos_ref, g_ref, temp, shift_b, True)
    dir_b[...] = pull(g_ref, a_b)


def next_kernel(
    ra, rb, a_b, b_b, dir_a_in, dir_b_in, sums_in, temp_ref, bias_ref,
    dir_a, dir_b, ra_b, rb_b, sums_ref, cos_ref, g_ref,
):
    temp, shift_b = temp_ref[0], bias_ref[0]
    sums = zero3()
    for raw, raw_b, own_b, start, out in (
        (ra, ra_b, a_b, dir_a_in, dir_a),
        (rb, rb_b, b_b, dir_b_in, dir_b),
    ):
        unit_into(raw_b, raw)
        cos_ref[...] = cosines(own_b[...], raw_b[...])
        sums = score_all(cos_ref, g_ref, temp, shift_b, False, sums)
        out[...] = start[...] + pull(g_ref, raw_b)
    sums_ref[...] = sums_in[...] + 0.5 * pack(sums)


def sums_kernel(
    ra2, rb2, a_b, b_b, ra_b, rb_b, sums_in, temp_ref, bias_ref, copies, far_b, cos_ref
):
    temp, shift_b = temp_ref[0], bias_ref[0]

    def run(far, own_b, near_b):
        unit_into(far_b, far)
        sums = zero3()
        for ref in (own_b, near_b):
            cos_ref[...] = cosines(ref[...], far_b[...])
            sums = score_all(cos_ref, None, temp, shift_b, False, sums)
        packed = sums_in[...] + pack(sums)
        for at in range(copies.shape[0]):
            copies[at] = packed

    even = is_even()
    pl.when(even)(lambda: run(rb2, b_b, ra_b))
    pl.when(jnp.logical_not(even))(lambda: run(ra2, a_b, rb_b))


def far_direction(dir_ref, start, own_b, raws, units, grads, cos_ref, temp, shift_b):
    for raw, unit_b, g_ref in zip(raws, units, grads):
        unit_into(unit_b, raw)
        cos_ref[...] = cosines(own_b[...], unit_b[...])
        score_all(cos_ref, g_ref, temp, shift_b)
    dir_ref[...] = start[...] + pull(grads[0], units[0]) + pull(grads[1], units[1])


def back_into(out_ref, own_ref, dir_ref, temp):
    for rows in chunks(out_ref, 32):
        wide = own_ref[rows, :].astype(F32)
        direction = dir_ref[rows, :]
        inverse = inverse_norm(wide)
        unit = wide * inverse
        along = jnp.sum(unit * direction, axis=1, keepdims=True)
        out_ref[rows, :] = ((direction - unit * along) * (temp * inverse)).astype(BF16)


def first_kernel(
    ra2, ra3, a, a_b, dir_a, temp_ref, bias_ref, grad_a,
    u2, u3, cos_ref, g2, g3, dir_ref,
):
    temp, shift_b = temp_ref[0], bias_ref[0]
    far_direction(dir_ref, dir_a, a_b, (ra2, ra3), (u2, u3), (g2, g3), cos_ref, temp, shift_b)
    back_into(grad_a, a, dir_ref, temp)


def second_kernel(
    rb2, rb3, b, b_b, dir_b, grad_a, temp_ref, bias_ref, image_grad, text_grad,
    u2, u3, cos_ref, g2, g3, dir_ref, grad_b, sem,
):
    temp, shift_b = temp_ref[0], bias_ref[0]
    far_direction(dir_ref, dir_b, b_b, (rb2, rb3), (u2, u3), (g2, g3), cos_ref, temp, shift_b)
    back_into(grad_b, b, dir_ref, temp)

    def move(first, second):
        copies = [
            pltpu.make_async_copy(grad_a, first, sem.at[0]),
            pltpu.make_async_copy(grad_b, second, sem.at[1]),
        ]
        for copy in copies:
            copy.start()
        for copy in copies:
            copy.wait()

    even = is_even()
    pl.when(even)(lambda: move(text_grad, image_grad))
    pl.when(jnp.logical_not(even))(lambda: move(image_grad, text_grad))


def add_parts(parts):
    packed = parts[0]
    for at in range(1, parts.shape[0]):
        packed = packed + parts[at]
    return packed


def relay_kernel(parts, copies):
    packed = add_parts(parts)
    for at in range(copies.shape[0]):
        copies[at] = packed


def finish_kernel(total, parts, temp_ref, loss, dtemp, dbias):
    packed = add_parts(parts)
    loss[0] = jnp.sum(packed[0:1, :]) / total
    dtemp[0] = temp_ref[0] * jnp.sum(packed[1:2, :]) / total
    dbias[0] = jnp.sum(packed[2:3, :]) / total


def call(kernel, ins, outs, out_specs, scratch=(), matmuls=0, spec=VMEM):
    specs = [SMEM if value.shape == (1,) else spec for value in ins]
    return pl.pallas_call(
        kernel,
        out_shape=outs,
        in_specs=specs,
        out_specs=out_specs,
        scratch_shapes=list(scratch),
        compiler_params=pltpu.CompilerParams(vmem_limit_bytes=12 * 2**20),
        cost_estimate=pl.CostEstimate(
            flops=matmuls * 2 * 256 * 256 * 1152, bytes_accessed=2**20, transcendentals=0
        ),
    )(*ins)


def per_device(images, texts, log_temp, bias):
    shape = images.shape
    rows = shape[0]
    total = rows * lax.axis_size(AXES)
    wide = jax.ShapeDtypeStruct(shape, F32)
    half = jax.ShapeDtypeStruct(shape, BF16)
    tile = jax.ShapeDtypeStruct((8, 128), F32)
    one = jax.ShapeDtypeStruct((1,), F32)
    unit, direction = pltpu.VMEM(shape, BF16), pltpu.VMEM(shape, F32)
    cos, grad = pltpu.VMEM((rows, rows), F32), pltpu.VMEM((rows, rows), BF16)
    pair_sem = pltpu.SemaphoreType.DMA((2,))
    temp = jnp.exp(log_temp)

    a, b = call(order_kernel, (images, texts), (half, half), (VMEM, VMEM), (pair_sem,), 0, ANY)
    ra, rb = swap_ahead(a), swap_across(b)
    own = call(
        own_kernel, (a, b, temp, bias), (half, half, wide, wide, tile), (VMEM,) * 5,
        (cos, grad), 8,
    )
    ra, (a_b, b_b, dir_a, dir_b, sums) = lax.optimization_barrier((ra, own))
    rb2 = swap_across(ra)
    ra2 = swap_ahead(rb)
    near = call(
        next_kernel, (ra, rb, a_b, b_b, dir_a, dir_b, sums, temp, bias),
        (wide, wide, half, half, tile), (VMEM,) * 5, (cos, grad), 8,
    )
    rb2, (dir_a, dir_b, ra_b, rb_b, sums) = lax.optimization_barrier((rb2, near))
    ra3 = swap_ahead(rb2)
    rb3 = swap_across(ra2)
    copies = call(
        sums_kernel, (ra2, rb2, a_b, b_b, ra_b, rb_b, sums, temp, bias),
        jax.ShapeDtypeStruct((lax.axis_size("blk"), 8, 128), F32), VMEM, (unit, cos), 4,
    )
    parts = lax.all_to_all(copies, "blk", 0, 0, tiled=True)
    scratch = (unit, unit, cos, grad, grad, direction)
    grad_a = call(first_kernel, (ra2, ra3, a, a_b, dir_a, temp, bias), half, VMEM, scratch, 8)
    parts, grad_a = lax.optimization_barrier((parts, grad_a))
    copies = call(
        relay_kernel, (parts,), jax.ShapeDtypeStruct((lax.axis_size("sub"), 8, 128), F32), VMEM
    )
    dir_b, _ = lax.optimization_barrier((dir_b, copies))
    parts = lax.all_to_all(copies, "sub", 0, 0, tiled=True)
    image_grad, text_grad = call(
        second_kernel, (rb2, rb3, b, b_b, dir_b, grad_a, temp, bias), (half, half), (ANY, ANY),
        scratch + (unit, pair_sem), 8,
    )
    loss, dtemp, dbias = call(
        functools.partial(finish_kernel, total), (parts, temp), (one,) * 3, (SMEM,) * 3
    )
    return (loss, image_grad, text_grad, dtemp, dbias)


def solution(mesh):
    in_specs = (P(AXES, None), P(AXES, None), P(), P())
    out_specs = (P(), P(AXES, None), P(AXES, None), P(), P())
    return jax.shard_map(
        per_device, mesh=mesh, in_specs=in_specs, out_specs=out_specs, check_vma=False
    )
```

```python
import functools

import jax
import jax.numpy as jnp
from jax import lax
from jax.experimental import pallas as pl
from jax.experimental.pallas import tpu as pltpu
from jax.sharding import PartitionSpec as P

AXES = ("blk", "sub")
ROWS = 64
VMEM = pl.BlockSpec(memory_space=pltpu.VMEM)
ANY = pl.BlockSpec(memory_space=pl.ANY)
SMEM = pl.BlockSpec(memory_space=pltpu.SMEM)
F32 = jnp.float32
BF16 = jnp.bfloat16


def swap_ahead(value):
    count = lax.axis_size(AXES)
    return lax.ppermute(value, AXES, [(at, at ^ 1) for at in range(count)])


def swap_across(value):
    count = lax.axis_size(AXES)
    pairs = [(at, (at - 1 if at % 2 == 0 else at + 1) % count) for at in range(count)]
    return lax.ppermute(value, AXES, pairs)


def is_even():
    return lax.axis_index("sub") % 2 == 0


def chunks(ref, size=ROWS):
    return [pl.ds(start, size) for start in range(0, ref.shape[0], size)]


def inverse_norm(wide):
    return 1.0 / jnp.sqrt(jnp.sum(wide * wide, axis=1, keepdims=True) + 1e-06)


def unit_into(out_ref, in_ref):
    for rows in chunks(in_ref, 32):
        wide = in_ref[rows, :].astype(F32)
        out_ref[rows, :] = (wide * inverse_norm(wide)).astype(BF16)


def cosines(left, right):
    return lax.dot_general(left, right, (((1,), (1,)), ((), ())), preferred_element_type=F32)


def score(cos, temp, shift_b, diagonal=None):
    z = temp * cos + shift_b
    if diagonal is not None:
        row = lax.broadcasted_iota(jnp.int32, z.shape, 0) + diagonal
        eye = row == lax.broadcasted_iota(jnp.int32, z.shape, 1)
        z = jnp.where(eye, -z, z)
    e = jnp.exp(-jnp.abs(z))
    r = 1.0 / (1.0 + e)
    grad = jnp.where(z >= 0, r, e * r)
    if diagonal is not None:
        grad = jnp.where(eye, -grad, grad)
    return cos, z, e, grad


def fold(values):
    rows = values.shape[0]
    part = jnp.sum(values.reshape(rows // 8, 8, values.shape[1]), axis=0)
    return sum(part[:, at : at + 128] for at in range(0, values.shape[1], 128))


def tally(cos, z, e, grad):
    rows, columns = e.shape
    factors = (1.0 + e).reshape(rows // 8, 8, columns)
    product = factors[0]
    for at in range(1, rows // 8):
        product = product * factors[at]
    return (
        fold(jnp.maximum(z, 0.0)) + fold(jnp.log(product)),
        fold(grad * cos),
        fold(grad),
    )


def add3(left, right):
    return tuple(a + b for a, b in zip(left, right))


def pack(sums):
    row = lax.broadcasted_iota(jnp.int32, (8, 128), 0)
    loss, dtemp, dbias = (jnp.sum(part, axis=0, keepdims=True) for part in sums)
    rest = jnp.where(row == 2, dbias, 0.0)
    return jnp.where(row == 0, loss, jnp.where(row == 1, dtemp, rest))


def one_row(packed):
    lane = lax.broadcasted_iota(jnp.int32, (1, 128), 1)
    sums = jnp.sum(packed, axis=1, keepdims=True)
    rest = jnp.where(lane == 2, sums[2:3], 0.0)
    return jnp.where(lane == 0, sums[0:1], jnp.where(lane == 1, sums[1:2], rest))


def zero3():
    return (jnp.zeros((8, 128), F32),) * 3


def score_all(cos_ref, g_ref, temp, shift_b, own=False, sums=None):
    for rows in chunks(cos_ref, ROWS):
        terms = score(cos_ref[rows, :], temp, shift_b, rows.start if own else None)
        if sums is not None:
            sums = add3(sums, tally(*terms))
        if g_ref is not None:
            g_ref[rows, :] = terms[3].astype(BF16)
    return sums


def pull(g_ref, other_ref):
    return jnp.dot(g_ref[...], other_ref[...], preferred_element_type=F32)


def order_kernel(images, texts, a, b, held, get_sem, put_sem):
    def move(first, second):
        half = a.shape[0] // 2
        copies = []
        for at in range(4):
            side, rows = at % 2, pl.ds(at // 2 * half, half)
            source, target = ((first, a), (second, b))[side]
            slot = held.at[side, rows]
            copies.append(
                (
                    pltpu.make_async_copy(source.at[rows], slot, get_sem.at[at]),
                    pltpu.make_async_copy(slot, target.at[rows], put_sem.at[at]),
                )
            )
        for get, _ in copies:
            get.start()
        for get, put in copies:
            get.wait()
            put.start()
        for _, put in copies:
            put.wait()

    even = is_even()
    pl.when(even)(lambda: move(texts, images))
    pl.when(jnp.logical_not(even))(lambda: move(images, texts))


def own_kernel(a, b, temp_ref, bias_ref, a_b, b_b, dir_a, dir_b, sums_ref, cos_ref, g_ref):
    temp, shift_b = temp_ref[0], bias_ref[0]
    unit_into(a_b, a)
    unit_into(b_b, b)
    cos_ref[...] = cosines(a_b[...], b_b[...])
    sums_ref[...] = pack(score_all(cos_ref, g_ref, temp, shift_b, True, zero3()))
    dir_a[...] = pull(g_ref, b_b)
    cos_ref[...] = cosines(b_b[...], a_b[...])
    score_all(cos_ref, g_ref, temp, shift_b, True)
    dir_b[...] = pull(g_ref, a_b)


def next_kernel(
    ra, rb, a_b, b_b, dir_a_in, dir_b_in, sums_in, temp_ref, bias_ref,
    dir_a, dir_b, ra_b, rb_b, sums_ref, cos_ref, g_ref,
):
    temp, shift_b = temp_ref[0], bias_ref[0]
    sums = zero3()
    for raw, raw_b, own_b, start, out in (
        (ra, ra_b, a_b, dir_a_in, dir_a),
        (rb, rb_b, b_b, dir_b_in, dir_b),
    ):
        unit_into(raw_b, raw)
        cos_ref[...] = cosines(own_b[...], raw_b[...])
        sums = score_all(cos_ref, g_ref, temp, shift_b, False, sums)
        out[...] = start[...] + pull(g_ref, raw_b)
    sums_ref[...] = sums_in[...] + 0.5 * pack(sums)


def sums_kernel(
    ra2, rb2, a_b, b_b, ra_b, rb_b, sums_in, temp_ref, bias_ref, copies, far_b, cos_ref
):
    temp, shift_b = temp_ref[0], bias_ref[0]

    def run(far, own_b, near_b):
        unit_into(far_b, far)
        sums = zero3()
        for ref in (own_b, near_b):
            cos_ref[...] = cosines(ref[...], far_b[...])
            sums = score_all(cos_ref, None, temp, shift_b, False, sums)
        packed = one_row(sums_in[...] + pack(sums))
        for at in range(copies.shape[0]):
            copies[at] = packed

    even = is_even()
    pl.when(even)(lambda: run(rb2, b_b, ra_b))
    pl.when(jnp.logical_not(even))(lambda: run(ra2, a_b, rb_b))


def far_direction(dir_ref, start, own_b, raws, units, grads, cos_ref, temp, shift_b):
    for raw, unit_b, g_ref in zip(raws, units, grads):
        unit_into(unit_b, raw)
        cos_ref[...] = cosines(own_b[...], unit_b[...])
        score_all(cos_ref, g_ref, temp, shift_b)
    dir_ref[...] = start[...] + pull(grads[0], units[0]) + pull(grads[1], units[1])


def back_into(out_ref, own_ref, dir_ref, temp):
    for rows in chunks(out_ref, 32):
        wide = own_ref[rows, :].astype(F32)
        direction = dir_ref[rows, :]
        inverse = inverse_norm(wide)
        unit = wide * inverse
        along = jnp.sum(unit * direction, axis=1, keepdims=True)
        out_ref[rows, :] = ((direction - unit * along) * (temp * inverse)).astype(BF16)


def first_kernel(
    ra2, ra3, a, a_b, dir_a, temp_ref, bias_ref, grad_a,
    u2, u3, cos_ref, g2, g3, dir_ref,
):
    temp, shift_b = temp_ref[0], bias_ref[0]
    far_direction(dir_ref, dir_a, a_b, (ra2, ra3), (u2, u3), (g2, g3), cos_ref, temp, shift_b)
    back_into(grad_a, a, dir_ref, temp)


def second_kernel(
    rb2, rb3, b, b_b, dir_b, grad_a, temp_ref, bias_ref, image_grad, text_grad,
    u2, u3, cos_ref, g2, g3, dir_ref, grad_b, sem,
):
    temp, shift_b = temp_ref[0], bias_ref[0]
    far_direction(dir_ref, dir_b, b_b, (rb2, rb3), (u2, u3), (g2, g3), cos_ref, temp, shift_b)
    back_into(grad_b, b, dir_ref, temp)

    def move(first, second):
        copies = [
            pltpu.make_async_copy(grad_a, first, sem.at[0]),
            pltpu.make_async_copy(grad_b, second, sem.at[1]),
        ]
        for copy in copies:
            copy.start()
        for copy in copies:
            copy.wait()

    even = is_even()
    pl.when(even)(lambda: move(text_grad, image_grad))
    pl.when(jnp.logical_not(even))(lambda: move(image_grad, text_grad))


def add_parts(parts):
    packed = parts[0]
    for at in range(1, parts.shape[0]):
        packed = packed + parts[at]
    return packed


def relay_kernel(parts, copies):
    packed = add_parts(parts)
    for at in range(copies.shape[0]):
        copies[at] = packed


def finish_kernel(total, parts, temp_ref, loss, dtemp, dbias):
    packed = add_parts(parts)
    lane = lax.broadcasted_iota(jnp.int32, packed.shape, 1)
    loss[0] = jnp.sum(jnp.where(lane == 0, packed, 0.0)) / total
    dtemp[0] = temp_ref[0] * jnp.sum(jnp.where(lane == 1, packed, 0.0)) / total
    dbias[0] = jnp.sum(jnp.where(lane == 2, packed, 0.0)) / total


def call(kernel, ins, outs, out_specs, scratch=(), matmuls=0, spec=VMEM, limit=12):
    specs = [SMEM if value.shape == (1,) else spec for value in ins]
    return pl.pallas_call(
        kernel,
        out_shape=outs,
        in_specs=specs,
        out_specs=out_specs,
        scratch_shapes=list(scratch),
        compiler_params=pltpu.CompilerParams(vmem_limit_bytes=limit * 2**20),
        cost_estimate=pl.CostEstimate(
            flops=matmuls * 2 * 256 * 256 * 1152, bytes_accessed=2**20, transcendentals=0
        ),
    )(*ins)


def per_device(images, texts, log_temp, bias):
    shape = images.shape
    rows = shape[0]
    total = rows * lax.axis_size(AXES)
    wide = jax.ShapeDtypeStruct(shape, F32)
    half = jax.ShapeDtypeStruct(shape, BF16)
    tile = jax.ShapeDtypeStruct((8, 128), F32)
    one = jax.ShapeDtypeStruct((1,), F32)
    unit, direction = pltpu.VMEM(shape, BF16), pltpu.VMEM(shape, F32)
    cos, grad = pltpu.VMEM((rows, rows), F32), pltpu.VMEM((rows, rows), BF16)
    pair_sem = pltpu.SemaphoreType.DMA((2,))
    temp = jnp.exp(log_temp)

    a, b = call(
        order_kernel, (images, texts), (half, half), (ANY, ANY),
        (
            pltpu.VMEM((2,) + shape, BF16),
            pltpu.SemaphoreType.DMA((4,)), pltpu.SemaphoreType.DMA((4,)),
        ),
        0, ANY, 56,
    )
    ra, rb = swap_ahead(a), swap_across(b)
    own = call(
        own_kernel, (a, b, temp, bias), (half, half, wide, wide, tile), (VMEM,) * 5,
        (cos, grad), 8,
    )
    ra, (a_b, b_b, dir_a, dir_b, sums) = lax.optimization_barrier((ra, own))
    rb2 = swap_across(ra)
    ra2 = swap_ahead(rb)
    near = call(
        next_kernel, (ra, rb, a_b, b_b, dir_a, dir_b, sums, temp, bias),
        (wide, wide, half, half, tile), (VMEM,) * 5, (cos, grad), 8,
    )
    rb2, (dir_a, dir_b, ra_b, rb_b, sums) = lax.optimization_barrier((rb2, near))
    ra3 = swap_ahead(rb2)
    rb3 = swap_across(ra2)
    copies = call(
        sums_kernel, (ra2, rb2, a_b, b_b, ra_b, rb_b, sums, temp, bias),
        jax.ShapeDtypeStruct((lax.axis_size("blk"), 1, 128), F32), VMEM, (unit, cos), 4,
    )
    parts = lax.all_to_all(copies, "blk", 0, 0, tiled=True)
    scratch = (unit, unit, cos, grad, grad, direction)
    grad_a = call(first_kernel, (ra2, ra3, a, a_b, dir_a, temp, bias), half, VMEM, scratch, 8)
    parts, grad_a = lax.optimization_barrier((parts, grad_a))
    copies = call(
        relay_kernel, (parts,), jax.ShapeDtypeStruct((lax.axis_size("sub"), 1, 128), F32), VMEM
    )
    dir_b, _ = lax.optimization_barrier((dir_b, copies))
    parts = lax.all_to_all(copies, "sub", 0, 0, tiled=True)
    image_grad, text_grad = call(
        second_kernel, (rb2, rb3, b, b_b, dir_b, grad_a, temp, bias), (half, half), (ANY, ANY),
        scratch + (unit, pair_sem), 8,
    )
    loss, dtemp, dbias = call(
        functools.partial(finish_kernel, total), (parts, temp), (one,) * 3, (SMEM,) * 3
    )
    return (loss, image_grad, text_grad, dtemp, dbias)


def solution(mesh):
    in_specs = (P(AXES, None), P(AXES, None), P(), P())
    out_specs = (P(), P(AXES, None), P(AXES, None), P(), P())
    return jax.shard_map(
        per_device, mesh=mesh, in_specs=in_specs, out_specs=out_specs, check_vma=False
    )
```

```python
import functools

import jax
import jax.numpy as jnp
from jax import lax
from jax.experimental import pallas as pl
from jax.experimental.pallas import tpu as pltpu
from jax.sharding import PartitionSpec as P

AXES = ("blk", "sub")
ROWS = 64
VMEM = pl.BlockSpec(memory_space=pltpu.VMEM)
ANY = pl.BlockSpec(memory_space=pl.ANY)
SMEM = pl.BlockSpec(memory_space=pltpu.SMEM)
F32 = jnp.float32
BF16 = jnp.bfloat16


def swap_ahead(value):
    count = lax.axis_size(AXES)
    return lax.ppermute(value, AXES, [(at, at ^ 1) for at in range(count)])


def swap_across(value):
    count = lax.axis_size(AXES)
    pairs = [(at, (at - 1 if at % 2 == 0 else at + 1) % count) for at in range(count)]
    return lax.ppermute(value, AXES, pairs)


def is_even():
    return lax.axis_index("sub") % 2 == 0


def chunks(ref, size=ROWS):
    return [pl.ds(start, size) for start in range(0, ref.shape[0], size)]


def inverse_norm(wide):
    return 1.0 / jnp.sqrt(jnp.sum(wide * wide, axis=1, keepdims=True) + 1e-06)


def unit_into(out_ref, in_ref):
    for rows in chunks(in_ref, 32):
        wide = in_ref[rows, :].astype(F32)
        out_ref[rows, :] = (wide * inverse_norm(wide)).astype(BF16)


def cosines(left, right):
    return lax.dot_general(left, right, (((1,), (1,)), ((), ())), preferred_element_type=F32)


def score(cos, temp, shift_b, diagonal=None):
    z = temp * cos + shift_b
    if diagonal is not None:
        row = lax.broadcasted_iota(jnp.int32, z.shape, 0) + diagonal
        eye = row == lax.broadcasted_iota(jnp.int32, z.shape, 1)
        z = jnp.where(eye, -z, z)
    e = jnp.exp(-jnp.abs(z))
    r = 1.0 / (1.0 + e)
    grad = jnp.where(z >= 0, r, e * r)
    if diagonal is not None:
        grad = jnp.where(eye, -grad, grad)
    return cos, z, e, grad


def fold(values):
    rows = values.shape[0]
    part = jnp.sum(values.reshape(rows // 8, 8, values.shape[1]), axis=0)
    return sum(part[:, at : at + 128] for at in range(0, values.shape[1], 128))


def tally(cos, z, e, grad):
    rows, columns = e.shape
    factors = (1.0 + e).reshape(rows // 8, 8, columns)
    product = factors[0]
    for at in range(1, rows // 8):
        product = product * factors[at]
    return (
        fold(jnp.maximum(z, 0.0)) + fold(jnp.log(product)),
        fold(grad * cos),
        fold(grad),
    )


def add3(left, right):
    return tuple(a + b for a, b in zip(left, right))


def pack(sums):
    row = lax.broadcasted_iota(jnp.int32, (8, 128), 0)
    loss, dtemp, dbias = (jnp.sum(part, axis=0, keepdims=True) for part in sums)
    rest = jnp.where(row == 2, dbias, 0.0)
    return jnp.where(row == 0, loss, jnp.where(row == 1, dtemp, rest))


def one_row(packed):
    lane = lax.broadcasted_iota(jnp.int32, (1, 128), 1)
    sums = jnp.sum(packed, axis=1, keepdims=True)
    rest = jnp.where(lane == 2, sums[2:3], 0.0)
    return jnp.where(lane == 0, sums[0:1], jnp.where(lane == 1, sums[1:2], rest))


def zero3():
    return (jnp.zeros((8, 128), F32),) * 3


def score_all(cos_ref, g_ref, temp, shift_b, own=False, sums=None):
    for rows in chunks(cos_ref, ROWS):
        terms = score(cos_ref[rows, :], temp, shift_b, rows.start if own else None)
        if sums is not None:
            sums = add3(sums, tally(*terms))
        if g_ref is not None:
            g_ref[rows, :] = terms[3].astype(BF16)
    return sums


def pull(g_ref, other_ref):
    return jnp.dot(g_ref[...], other_ref[...], preferred_element_type=F32)


def order_kernel(images, texts, a, b, held, get_sem, put_sem):
    def move(first, second):
        half = a.shape[0] // 2
        copies = []
        for at in range(4):
            side, rows = at % 2, pl.ds(at // 2 * half, half)
            source, target = ((first, a), (second, b))[side]
            slot = held.at[side, rows]
            copies.append(
                (
                    pltpu.make_async_copy(source.at[rows], slot, get_sem.at[at]),
                    pltpu.make_async_copy(slot, target.at[rows], put_sem.at[at]),
                )
            )
        for get, _ in copies:
            get.start()
        for get, put in copies:
            get.wait()
            put.start()
        for _, put in copies:
            put.wait()

    even = is_even()
    pl.when(even)(lambda: move(texts, images))
    pl.when(jnp.logical_not(even))(lambda: move(images, texts))


def own_kernel(a, b, temp_ref, bias_ref, a_b, b_b, dir_a, dir_b, sums_ref, cos_ref, g_ref):
    temp, shift_b = temp_ref[0], bias_ref[0]
    unit_into(a_b, a)
    unit_into(b_b, b)
    cos_ref[...] = cosines(a_b[...], b_b[...])
    sums_ref[...] = pack(score_all(cos_ref, g_ref, temp, shift_b, True, zero3()))
    dir_a[...] = pull(g_ref, b_b)
    cos_ref[...] = cosines(b_b[...], a_b[...])
    score_all(cos_ref, g_ref, temp, shift_b, True)
    dir_b[...] = pull(g_ref, a_b)


def next_kernel(
    ra, rb, a_b, b_b, dir_a_in, dir_b_in, sums_in, temp_ref, bias_ref,
    dir_a, dir_b, ra_b, rb_b, sums_ref, cos_ref, g_ref,
):
    temp, shift_b = temp_ref[0], bias_ref[0]
    sums = zero3()
    for raw, raw_b, own_b, start, out in (
        (ra, ra_b, a_b, dir_a_in, dir_a),
        (rb, rb_b, b_b, dir_b_in, dir_b),
    ):
        unit_into(raw_b, raw)
        cos_ref[...] = cosines(own_b[...], raw_b[...])
        sums = score_all(cos_ref, g_ref, temp, shift_b, False, sums)
        out[...] = start[...] + pull(g_ref, raw_b)
    sums_ref[...] = sums_in[...] + 0.5 * pack(sums)


def sums_kernel(
    ra2, rb2, a_b, b_b, ra_b, rb_b, sums_in, temp_ref, bias_ref, copies, far_b, cos_ref
):
    temp, shift_b = temp_ref[0], bias_ref[0]

    def run(far, own_b, near_b):
        unit_into(far_b, far)
        sums = zero3()
        for ref in (own_b, near_b):
            cos_ref[...] = cosines(ref[...], far_b[...])
            sums = score_all(cos_ref, None, temp, shift_b, False, sums)
        packed = one_row(sums_in[...] + pack(sums))
        for at in range(copies.shape[0]):
            copies[at] = packed

    even = is_even()
    pl.when(even)(lambda: run(rb2, b_b, ra_b))
    pl.when(jnp.logical_not(even))(lambda: run(ra2, a_b, rb_b))


def far_direction(dir_ref, start, own_b, raws, units, grads, cos_ref, temp, shift_b):
    for raw, unit_b, g_ref in zip(raws, units, grads):
        unit_into(unit_b, raw)
        cos_ref[...] = cosines(own_b[...], unit_b[...])
        score_all(cos_ref, g_ref, temp, shift_b)
    dir_ref[...] = start[...] + pull(grads[0], units[0]) + pull(grads[1], units[1])


def back_into(out_ref, own_ref, dir_ref, temp):
    for rows in chunks(out_ref, 32):
        wide = own_ref[rows, :].astype(F32)
        direction = dir_ref[rows, :]
        inverse = inverse_norm(wide)
        unit = wide * inverse
        along = jnp.sum(unit * direction, axis=1, keepdims=True)
        out_ref[rows, :] = ((direction - unit * along) * (temp * inverse)).astype(BF16)


def first_kernel(
    ra2, ra3, a, a_b, dir_a, temp_ref, bias_ref, grad_a,
    u2, u3, cos_ref, g2, g3, dir_ref,
):
    temp, shift_b = temp_ref[0], bias_ref[0]
    far_direction(dir_ref, dir_a, a_b, (ra2, ra3), (u2, u3), (g2, g3), cos_ref, temp, shift_b)
    back_into(grad_a, a, dir_ref, temp)


def second_kernel(
    rb2, rb3, b, b_b, dir_b, grad_a, temp_ref, bias_ref, image_grad, text_grad,
    u2, u3, cos_ref, g2, g3, dir_ref, grad_b, sem,
):
    temp, shift_b = temp_ref[0], bias_ref[0]
    far_direction(dir_ref, dir_b, b_b, (rb2, rb3), (u2, u3), (g2, g3), cos_ref, temp, shift_b)
    back_into(grad_b, b, dir_ref, temp)

    def move(first, second):
        copies = [
            pltpu.make_async_copy(grad_a, first, sem.at[0]),
            pltpu.make_async_copy(grad_b, second, sem.at[1]),
        ]
        for copy in copies:
            copy.start()
        for copy in copies:
            copy.wait()

    even = is_even()
    pl.when(even)(lambda: move(text_grad, image_grad))
    pl.when(jnp.logical_not(even))(lambda: move(image_grad, text_grad))


def add_parts(parts):
    packed = parts[0]
    for at in range(1, parts.shape[0]):
        packed = packed + parts[at]
    return packed


def relay_kernel(parts, copies):
    packed = add_parts(parts)
    for at in range(copies.shape[0]):
        copies[at] = packed


def finish_kernel(total, parts, temp_ref, loss, dtemp, dbias):
    packed = add_parts(parts)
    lane = lax.broadcasted_iota(jnp.int32, packed.shape, 1)
    loss[0] = jnp.sum(jnp.where(lane == 0, packed, 0.0)) / total
    dtemp[0] = temp_ref[0] * jnp.sum(jnp.where(lane == 1, packed, 0.0)) / total
    dbias[0] = jnp.sum(jnp.where(lane == 2, packed, 0.0)) / total


def call(kernel, ins, outs, out_specs, scratch=(), matmuls=0, spec=VMEM, limit=12):
    specs = [SMEM if value.shape == (1,) else spec for value in ins]
    return pl.pallas_call(
        kernel,
        out_shape=outs,
        in_specs=specs,
        out_specs=out_specs,
        scratch_shapes=list(scratch),
        compiler_params=pltpu.CompilerParams(vmem_limit_bytes=limit * 2**20),
        cost_estimate=pl.CostEstimate(
            flops=matmuls * 2 * 256 * 256 * 1152, bytes_accessed=2**20, transcendentals=0
        ),
    )(*ins)


def per_device(images, texts, log_temp, bias):
    shape = images.shape
    rows = shape[0]
    total = rows * lax.axis_size(AXES)
    wide = jax.ShapeDtypeStruct(shape, F32)
    half = jax.ShapeDtypeStruct(shape, BF16)
    tile = jax.ShapeDtypeStruct((8, 128), F32)
    one = jax.ShapeDtypeStruct((1,), F32)
    unit, direction = pltpu.VMEM(shape, BF16), pltpu.VMEM(shape, F32)
    cos, grad = pltpu.VMEM((rows, rows), F32), pltpu.VMEM((rows, rows), BF16)
    pair_sem = pltpu.SemaphoreType.DMA((2,))
    temp = jnp.exp(log_temp)

    a, b = call(
        order_kernel, (images, texts), (half, half), (ANY, ANY),
        (
            pltpu.VMEM((2,) + shape, BF16),
            pltpu.SemaphoreType.DMA((4,)), pltpu.SemaphoreType.DMA((4,)),
        ),
        0, ANY, 56,
    )
    rb = swap_across(b)
    ra = swap_ahead(a)
    own = call(
        own_kernel, (a, b, temp, bias), (half, half, wide, wide, tile), (VMEM,) * 5,
        (cos, grad), 8,
    )
    rb, (a_b, b_b, dir_a, dir_b, sums) = lax.optimization_barrier((rb, own))
    ra2 = swap_ahead(rb)
    rb2 = swap_across(ra)
    near = call(
        next_kernel, (ra, rb, a_b, b_b, dir_a, dir_b, sums, temp, bias),
        (wide, wide, half, half, tile), (VMEM,) * 5, (cos, grad), 8,
    )
    ra2, (dir_a, dir_b, ra_b, rb_b, sums) = lax.optimization_barrier((ra2, near))
    rb3 = swap_across(ra2)
    ra3 = swap_ahead(rb2)
    copies = call(
        sums_kernel, (ra2, rb2, a_b, b_b, ra_b, rb_b, sums, temp, bias),
        jax.ShapeDtypeStruct((lax.axis_size("blk"), 1, 128), F32), VMEM, (unit, cos), 4,
    )
    parts = lax.all_to_all(copies, "blk", 0, 0, tiled=True)
    scratch = (unit, unit, cos, grad, grad, direction)
    grad_a = call(first_kernel, (ra2, ra3, a, a_b, dir_a, temp, bias), half, VMEM, scratch, 8)
    parts, grad_a = lax.optimization_barrier((parts, grad_a))
    copies = call(
        relay_kernel, (parts,), jax.ShapeDtypeStruct((lax.axis_size("sub"), 1, 128), F32), VMEM
    )
    dir_b, _ = lax.optimization_barrier((dir_b, copies))
    parts = lax.all_to_all(copies, "sub", 0, 0, tiled=True)
    image_grad, text_grad = call(
        second_kernel, (rb2, rb3, b, b_b, dir_b, grad_a, temp, bias), (half, half), (ANY, ANY),
        scratch + (unit, pair_sem), 8,
    )
    loss, dtemp, dbias = call(
        functools.partial(finish_kernel, total), (parts, temp), (one,) * 3, (SMEM,) * 3
    )
    return (loss, image_grad, text_grad, dtemp, dbias)


def solution(mesh):
    in_specs = (P(AXES, None), P(AXES, None), P(), P())
    out_specs = (P(), P(AXES, None), P(AXES, None), P(), P())
    return jax.shard_map(
        per_device, mesh=mesh, in_specs=in_specs, out_specs=out_specs, check_vma=False
    )
```
